32 devices in a mesh: groups: 2 (over y), blk: 4 (over z), rep: 2 (over x), sub: 2 (over core).
Axes of the slice: x: 2, y: 2, z: 4, core: 2. Of those that a mesh axis runs over, the one named last changes fastest.
Arguments:
- out_grad: bfloat16 [16384, 256], P(('groups', 'blk', 'rep', 'sub')), parts along dimension 0, may hold values from -6 to 6
- pre_act: bfloat16 [16384, 256], P(('groups', 'blk', 'rep', 'sub')), parts along dimension 0, may hold values from -6 to 6
- features: bfloat16 [16384, 256], P(('groups', 'blk', 'rep', 'sub')), parts along dimension 0, may hold values from -0.15625 to 0.15625
- weight: bfloat16 [256, 256], replicated, may hold values from -0.375 to 0.375
- prop_tiles: bfloat16 [2048, 128, 128], P(('groups', 'blk', 'rep', 'sub')), parts along dimension 0, may hold values from -0.21875 to 0.21875
- tile_rows: int32 [2048], P(('groups', 'blk', 'rep', 'sub')), parts along dimension 0, may hold values from 0 to 15, as said below
- tile_cols: int32 [2048], P(('groups', 'blk', 'rep', 'sub')), parts along dimension 0, may hold values from 0 to 3
- tile_counts: int32 [128], P(('groups', 'blk', 'rep', 'sub')), parts along dimension 0, may hold values from 1 to 16, as said below
Outputs:
- feature_gradient: bfloat16 [16384, 256], P(('groups', 'blk', 'rep', 'sub')), parts along dimension 0
- grad_weight: float32 [512, 256], P('groups'), parts along dimension 0
The draws below stay inside these ranges and needn't reach their ends.
There are 2 independent parts, one for each index of `groups`. The reference program is written for one: setup_inputs(seed, part) draws one part's arguments, and reference() takes and returns one part's arrays. A program takes and returns all parts, laid end to end along the dimension named above; an argument that names none is the same for every part. Nothing has to cross between parts.
Inputs may be any that keep to these rules, and one draw needn't show every extreme that they name: Within each group of 16 slots the pairs (tile_rows, tile_cols) differ. `tile_counts`: slots of a group at or beyond its count are ignored; every index d has a group with 16 live slots.
All inputs are finite; a program needn't handle non-finite values.
Results may differ from the reference program's by a relative error of at most 0.0051.
Values may be sent and summed in bfloat16 or wider, within the bound.
A program may use at most 64 MiB of HBM per device.

```python
import jax
import jax.numpy as jnp
from jax import lax

F = 256
F_IN = 256
TILE = 128
CAP = 16
ROWS_DEV = 512
NODES = 8192
STRIP_TILES = 16
SHARD_TILES = 4
SLOTS = 1024
N_BLK = 4
N_REP = 2
N_SUB = 2


def tile_pairs(key):
    combos = STRIP_TILES * SHARD_TILES
    group_aggregate = N_BLK * N_REP * N_SUB * N_BLK
    keys = jax.random.split(key, group_aggregate)

    def pick_pairs(single):
        return jax.random.permutation(single, combos)[:CAP]
    chosen = jax.vmap(pick_pairs)(keys)
    return chosen.reshape(-1).astype(jnp.int32)


def draw_tile_rows(key, part):
    flat = tile_pairs(key)
    return (flat // SHARD_TILES).astype(jnp.int32)


def draw_tile_cols(key, part):
    flat = tile_pairs(key)
    return (flat % SHARD_TILES).astype(jnp.int32)


def draw_tile_counts(key, part):
    key = jax.random.fold_in(key, 23)
    device_total = N_BLK * N_REP * N_SUB
    key_heavy, key_raw, key_full = jax.random.split(key, 3)
    heavy = jax.random.randint(key_heavy, (device_total, 1), 1, 5)
    limit = jnp.maximum(1, CAP * heavy // 4)
    raw_counts = jax.random.randint(key_raw, (device_total, N_BLK), 0, 1 << 20) % limit + 1
    full_group = jax.random.randint(key_full, (device_total, 1), 0, N_BLK)
    positions = jnp.arange(N_BLK, dtype=jnp.int32)[None, :]
    counts = jnp.where(positions == full_group, CAP, raw_counts)
    return counts.reshape(-1).astype(jnp.int32)


def block_levels(own_key, shape, cuts, low, largest):
    gain, own = 1.0, jax.random.fold_in(own_key, 6)
    for position, blocks in cuts:
        steps = jnp.exp(jax.random.uniform(jax.random.fold_in(own, position), (blocks,), jnp.float32, low / len(cuts), largest / len(cuts)))
        gain = gain * jnp.repeat(steps, shape[position] // blocks).reshape([-1 if axis == position else 1 for axis in range(len(shape))])
    return gain


def bell_draw(rng, extent, scale, bound, cuts=(), kind=jnp.bfloat16):
    gain = block_levels(rng, extent, cuts, -0.22, 0.18) if cuts else 1.0
    entries = jax.random.normal(rng, extent, jnp.float32) * scale * gain
    return jnp.minimum(jnp.maximum(entries, -bound), bound).astype(kind)


def setup_inputs(seed: int = 0, part: int = 0) -> dict:
    streams_of = jax.random.split(jax.random.key(seed), 9)
    part_keys = jax.random.split(jax.random.fold_in(streams_of[8], part), 9)
    return {
        "out_grad": bell_draw(part_keys[0], (NODES, F), 1.0, 6.0, ((0, 16),)),
        "pre_act": bell_draw(part_keys[1], (NODES, F), 1.0, 6.0, ((0, 16),)),
        "features": bell_draw(part_keys[2], (NODES, F_IN), (1.0 / NODES ** 0.5), 0.15625, ((0, 16),)),
        "weight": bell_draw(streams_of[3], (F_IN, F), F ** -0.5, 0.375),
        "prop_tiles": bell_draw(part_keys[4], (SLOTS, TILE, TILE), (N_BLK * CAP * TILE * TILE // (3 * ROWS_DEV)) ** -0.5, 0.21875, ((0, 16),)),
        "tile_rows": draw_tile_rows(jax.random.fold_in(jax.random.fold_in(streams_of[8], part), 71), part),
        "tile_cols": draw_tile_cols(jax.random.fold_in(jax.random.fold_in(streams_of[8], part), 71), part),
        "tile_counts": draw_tile_counts(jax.random.fold_in(jax.random.fold_in(streams_of[8], part), 71), part),
    }


def reference(out_grad, pre_act, features, weight, prop_tiles, tile_rows, tile_cols, tile_counts):
    masked = jnp.where(pre_act > 0, out_grad, jnp.zeros_like(out_grad))
    members = N_REP * N_SUB
    width = masked.shape[1]
    shards = masked.reshape(N_BLK * members, SHARD_TILES, TILE, width)

    def single_band(strip):
        def add_member(running, member):
            device_index = strip * members + member

            def add_group(inner, group):
                first_slot = (device_index * N_BLK + group) * CAP
                adjacency_block = lax.dynamic_slice_in_dim(prop_tiles, first_slot, CAP, 0).astype(jnp.float32)
                row_index = lax.dynamic_slice_in_dim(tile_rows, first_slot, CAP, 0)
                col_index = lax.dynamic_slice_in_dim(tile_cols, first_slot, CAP, 0)
                active_count = tile_counts[device_index * N_BLK + group]
                source = shards[group * members + member]
                matmul_argument = source[col_index].astype(jnp.float32)
                block_product = jnp.einsum("giy,gym->gim", adjacency_block, matmul_argument)
                live_mask = (jnp.arange(CAP, dtype=jnp.int32) < active_count).astype(jnp.float32)
                return inner.at[row_index].add(block_product * live_mask[:, None, None]), None

            running, _ = lax.scan(add_group, running, jnp.arange(N_BLK, dtype=jnp.int32))
            return running, None

        zeroed = jnp.zeros((STRIP_TILES, TILE, width), jnp.float32)
        running, _ = lax.scan(add_member, zeroed, jnp.arange(members, dtype=jnp.int32))
        return running

    strips = lax.map(single_band, jnp.arange(N_BLK, dtype=jnp.int32))
    propagated_gradient = strips.reshape(NODES, width).astype(jnp.bfloat16)
    feature_gradient = jnp.dot(propagated_gradient, weight.T, preferred_element_type=jnp.float32).astype(jnp.bfloat16)
    grad_weight = jnp.dot(features.T, propagated_gradient, preferred_element_type=jnp.float32)
    return feature_gradient, grad_weight
```

```python
import functools

import jax
import jax.numpy as jnp
from jax import lax
from jax.experimental import pallas as pl
from jax.experimental.pallas import tpu as pltpu
from jax.sharding import PartitionSpec as P

TILE = 128
CAP = 16
HALF = 128
MESH = pl.DeviceIdType.MESH
BF16 = jnp.bfloat16
F32 = jnp.float32
SUB_WIRE = jnp.float32
KEEP_BYTES = 16 << 20


def kernel(n, n_rep, n_sub, halves, keep,
           og, pa, tr, tc, cnt, feat_any, w_any, tiles_any,
           fg, gw,
           gath, dense, tiles, inv_v, inv_s, part, sub_out, sub_in, rep_out, rep_in, acc, prop,
           feat, w, gwl, g1_out, g1_in, zbuf, gfin,
           loc_sem, ssem, rsem, sub_ss, sub_rs, rep_ss, rep_rs, g1_ss, g1_rs, z_ss, z_rs, f_ss, f_rs):
    rows = og.shape[0]
    slots = tiles_any.shape[0]
    shard = rows // TILE
    members = n_rep * n_sub
    strip = members * rows
    strip_tiles = strip // TILE
    b = lax.axis_index("blk")
    r = lax.axis_index("rep")
    s = lax.axis_index("sub")
    m = r * n_sub + s
    piece = gwl.shape[0] // members

    def member(t):
        return {"rep": t // n_sub, "sub": lax.rem(t, n_sub)}

    barrier = pltpu.get_barrier_semaphore()
    for o in range(1, n):
        pl.semaphore_signal(barrier, inc=1, device_id={"blk": lax.rem(b + o, n)}, device_id_type=MESH)
    for o in range(1, members):
        pl.semaphore_signal(barrier, inc=1, device_id=member(lax.rem(m + o, members)), device_id_type=MESH)

    tiles_copy = pltpu.make_async_copy(tiles_any, tiles.at[pl.ds(0, slots)], loc_sem.at[0])
    feat_copy = pltpu.make_async_copy(feat_any, feat, loc_sem.at[1])
    w_copy = pltpu.make_async_copy(w_any, w, loc_sem.at[2])
    tiles_copy.start()
    feat_copy.start()
    w_copy.start()

    for c in range(halves):
        cols = pl.ds(c * HALF, HALF)
        x = og[:, cols]
        gath[b, c] = jnp.where(pa[:, cols] > 0, x, jnp.zeros_like(x))

    def block_copy(c, origin, way):
        return pltpu.make_async_remote_copy(
            src_ref=gath.at[origin, c], dst_ref=gath.at[origin, c],
            send_sem=ssem.at[way, origin, c], recv_sem=rsem.at[origin, c],
            device_id={"blk": jnp.clip(b + (1 if way else -1), 0, n - 1)}, device_id_type=MESH)

    def send(c, origin, way):
        @pl.when((b + 1 < n) if way else (b > 0))
        def _():
            block_copy(c, origin, way).start()

    pl.semaphore_wait(barrier, n - 1 + members - 1)
    send(0, b, 0)
    send(0, b, 1)

    lane = lax.broadcasted_iota(jnp.int32, (1, inv_v.shape[1]), 1)

    def invert(g, carry):
        v = jnp.full((1, inv_v.shape[1]), slots, jnp.int32)
        for k in range(CAP):
            slot = g * CAP + k
            key = jnp.where(k < cnt[g], tr[slot] * shard + tc[slot], -1)
            v = jnp.where(lane == key, slot, v)
        inv_v[pl.ds(g, 1), :] = v
        return carry

    lax.fori_loop(0, n, invert, 0)
    inv_copy = pltpu.make_async_copy(inv_v, inv_s, loc_sem.at[3])
    inv_copy.start()
    tiles[slots] = jnp.zeros((TILE, TILE), BF16)
    inv_copy.wait()
    tiles_copy.wait()

    def build(g):
        where = g if keep else 0

        def one(t, carry):
            for c in range(shard):
                index = inv_s[g, t * shard + c]
                dense[where, pl.ds(pl.multiple_of(t * TILE, TILE), TILE), pl.ds(c * TILE, TILE)] = tiles[index]
            return carry

        lax.fori_loop(0, strip_tiles, one, 0)

    def accumulate(g, c, first):
        where = g if keep else 0
        if c == 0 or not keep:
            build(g)
        step = 512

        def one(t, carry):
            at = pl.ds(pl.multiple_of(t * step, step), step)
            product = jnp.dot(dense[where, at, :], gath[g, c], preferred_element_type=F32)
            if first:
                part[c, at, :] = product
            else:
                part[c, at, :] += product
            return carry

        lax.fori_loop(0, strip // step, one, 0)

    def gather(c, low, high):
        def one(d, carry):
            @pl.when(b - d >= 0)
            def _():
                block_copy(c, b - d, 1).wait_recv()
                send(c, b - d, 1)

            @pl.when(b + d < n)
            def _():
                block_copy(c, b + d, 0).wait_recv()
                send(c, b + d, 0)

            if c + 1 < halves:
                @pl.when(d == 1)
                def _():
                    send(c + 1, b, 0)
                    send(c + 1, b, 1)

            @pl.when(b - d >= 0)
            def _():
                accumulate(b - d, c, False)

            @pl.when(b + d < n)
            def _():
                accumulate(b + d, c, False)
            return carry

        if low < high:
            lax.fori_loop(low, high, one, 0)

    def sub_copy(c, o):
        return pltpu.make_async_remote_copy(
            src_ref=sub_out.at[c, o - 1], dst_ref=sub_in.at[c, o - 1],
            send_sem=sub_ss.at[c, o - 1], recv_sem=sub_rs.at[c, o - 1],
            device_id={"sub": lax.rem(s + o, n_sub)}, device_id_type=MESH)

    def rep_copy(c, o):
        return pltpu.make_async_remote_copy(
            src_ref=rep_out.at[c, o - 1], dst_ref=rep_in.at[c, o - 1],
            send_sem=rep_ss.at[c, o - 1], recv_sem=rep_rs.at[c, o - 1],
            device_id={"rep": lax.rem(r + o, n_rep)}, device_id_type=MESH)

    def block_rows(t):
        return pl.ds(pl.multiple_of(t * rows, rows), rows)

    def sub_stage(c):
        for o in range(1, n_sub):
            t = lax.rem(s + o, n_sub)
            for q in range(n_rep):
                sub_out[c, o - 1, pl.ds(q * rows, rows), :] = part[c, block_rows(q * n_sub + t), :].astype(SUB_WIRE)
            sub_copy(c, o).start()

    def rep_stage(c):
        for o in range(1, n_sub):
            sub_copy(c, o).wait_recv()

        def summed(t):
            total = part[c, block_rows(t * n_sub + s), :]
            for o in range(1, n_sub):
                total = total + sub_in[c, o - 1, block_rows(t), :].astype(F32)
            return total

        for o in range(1, n_rep):
            rep_out[c, o - 1] = summed(lax.rem(r + o, n_rep)).astype(BF16)
            rep_copy(c, o).start()
        acc[c] = summed(r)

    def prop_stage(c):
        for o in range(1, n_rep):
            rep_copy(c, o).wait_recv()
        total = acc[c]
        for o in range(1, n_rep):
            total = total + rep_in[c, o - 1].astype(F32)
        prop[c] = total.astype(BF16)

    def weight_term(c):
        gwl[:, pl.ds(c * HALF, HALF)] = lax.dot_general(
            feat[...], prop[c], (((0,), (0,)), ((), ())), preferred_element_type=F32)

    accumulate(b, 0, True)
    gather(0, 1, n)
    for c in range(halves):
        sub_stage(c)
        if c + 1 < halves:
            accumulate(b, c + 1, True)
            gather(c + 1, 1, 2)
            rep_stage(c)
            gather(c + 1, 2, 3)
            prop_stage(c)
            if c == 0:
                feat_copy.wait()
                w_copy.wait()
            weight_term(c)
            gather(c + 1, 3, n)
        else:
            rep_stage(c)
            prop_stage(c)
            weight_term(c)

    def g1_copy(o):
        return pltpu.make_async_remote_copy(
            src_ref=g1_out.at[o - 1], dst_ref=g1_in.at[o - 1],
            send_sem=g1_ss.at[o - 1], recv_sem=g1_rs.at[o - 1],
            device_id=member(lax.rem(m + o, members)), device_id_type=MESH)

    def z_copy(o, origin):
        return pltpu.make_async_remote_copy(
            src_ref=zbuf.at[origin], dst_ref=zbuf.at[origin],
            send_sem=z_ss.at[o - 1], recv_sem=z_rs.at[origin],
            device_id={"blk": lax.rem(b + o, n)}, device_id_type=MESH)

    def f_copy(o, origin):
        return pltpu.make_async_remote_copy(
            src_ref=gfin.at[origin], dst_ref=gfin.at[origin],
            send_sem=f_ss.at[o - 1], recv_sem=f_rs.at[origin],
            device_id=member(lax.rem(m + o, members)), device_id_type=MESH)

    def piece_rows(t):
        return pl.ds(pl.multiple_of(t * piece, piece), piece)

    for o in range(1, members):
        g1_out[o - 1] = gwl[piece_rows(lax.rem(m + o, members)), :].astype(BF16)
        g1_copy(o).start()

    total = None
    for c in range(halves):
        term = lax.dot_general(prop[c], w[:, pl.ds(c * HALF, HALF)], (((1,), (1,)), ((), ())),
                               preferred_element_type=F32)
        total = term if total is None else total + term
    fg[...] = total.astype(BF16)

    for o in range(1, members):
        g1_copy(o).wait_recv()
    total = gwl[piece_rows(m), :]
    for o in range(1, members):
        total = total + g1_in[o - 1].astype(F32)
    zbuf[b] = total.astype(BF16)
    for o in range(1, n):
        z_copy(o, b).start()
    for o in range(1, n):
        z_copy(o, lax.rem(b + o, n)).wait_recv()
    total = zbuf[0].astype(F32)
    for q in range(1, n):
        total = total + zbuf[q].astype(F32)
    gfin[m] = total.astype(BF16)
    for o in range(1, members):
        f_copy(o, m).start()
    for o in range(1, members):
        f_copy(o, lax.rem(m + o, members)).wait_recv()
    for q in range(members):
        gw[pl.ds(q * piece, piece), :] = gfin[q].astype(F32)

    def drain(origin, carry):
        for c in range(halves):
            @pl.when((origin <= b) & (b + 1 < n))
            def _():
                block_copy(c, origin, 1).wait_send()

            @pl.when((origin >= b) & (b > 0))
            def _():
                block_copy(c, origin, 0).wait_send()
        return carry

    lax.fori_loop(0, n, drain, 0)
    for c in range(halves):
        for o in range(1, n_sub):
            sub_copy(c, o).wait_send()
        for o in range(1, n_rep):
            rep_copy(c, o).wait_send()
    for o in range(1, members):
        g1_copy(o).wait_send()
        f_copy(o, m).wait_send()
    for o in range(1, n):
        z_copy(o, b).wait_send()


def local(n, n_rep, n_sub, out_grad, pre_act, features, weight, prop_tiles, tile_rows, tile_cols, tile_counts):
    rows, width = out_grad.shape
    f_in = features.shape[1]
    slots = prop_tiles.shape[0]
    halves = width // HALF
    members = n_rep * n_sub
    strip = members * rows
    keep = n * strip * rows * 2 <= KEEP_BYTES
    lanes = -(-(strip // TILE) * (rows // TILE) // 128) * 128
    inv_shape = (-(-n // 8) * 8, lanes)
    piece = f_in // members
    dma = pltpu.SemaphoreType.DMA
    vmem = pl.BlockSpec(memory_space=pltpu.VMEM)
    smem = pl.BlockSpec(memory_space=pltpu.SMEM)
    hbm = pl.BlockSpec(memory_space=pl.ANY)
    subs, reps = max(n_sub - 1, 1), max(n_rep - 1, 1)
    return pl.pallas_call(
        functools.partial(kernel, n, n_rep, n_sub, halves, keep),
        out_shape=(
            jax.ShapeDtypeStruct((rows, weight.shape[0]), BF16),
            jax.ShapeDtypeStruct((f_in, width), F32),
        ),
        in_specs=[vmem, vmem, smem, smem, smem, hbm, hbm, hbm],
        out_specs=(vmem, vmem),
        scratch_shapes=[
            pltpu.VMEM((n, halves, rows, HALF), BF16),
            pltpu.VMEM((n if keep else 1, strip, rows), BF16),
            pltpu.VMEM((slots + 1, TILE, TILE), BF16),
            pltpu.VMEM(inv_shape, jnp.int32),
            pltpu.SMEM(inv_shape, jnp.int32),
            pltpu.VMEM((halves, strip, HALF), F32),
            pltpu.VMEM((halves, subs, n_rep * rows, HALF), SUB_WIRE),
            pltpu.VMEM((halves, subs, n_rep * rows, HALF), SUB_WIRE),
            pltpu.VMEM((halves, reps, rows, HALF), BF16),
            pltpu.VMEM((halves, reps, rows, HALF), BF16),
            pltpu.VMEM((halves, rows, HALF), F32),
            pltpu.VMEM((halves, rows, HALF), BF16),
            pltpu.VMEM(features.shape, BF16),
            pltpu.VMEM(weight.shape, BF16),
            pltpu.VMEM((f_in, width), F32),
            pltpu.VMEM((members - 1, piece, width), BF16),
            pltpu.VMEM((members - 1, piece, width), BF16),
            pltpu.VMEM((n, piece, width), BF16),
            pltpu.VMEM((members, piece, width), BF16),
            dma((4,)),
            dma((2, n, halves)),
            dma((n, halves)),
            dma((halves, subs)),
            dma((halves, subs)),
            dma((halves, reps)),
            dma((halves, reps)),
            dma((members - 1,)),
            dma((members - 1,)),
            dma((n - 1,)),
            dma((n,)),
            dma((members - 1,)),
            dma((members,)),
        ],
        compiler_params=pltpu.CompilerParams(
            collective_id=0, has_side_effects=True, vmem_limit_bytes=48 << 20),
    )(out_grad, pre_act, tile_rows, tile_cols, tile_counts, features, weight, prop_tiles)


def solution(mesh):
    placed = P(("groups", "blk", "rep", "sub"))
    return jax.shard_map(
        functools.partial(local, mesh.shape["blk"], mesh.shape["rep"], mesh.shape["sub"]),
        mesh=mesh,
        in_specs=(placed, placed, placed, P(), placed, placed, placed, placed),
        out_specs=(placed, P("groups", None)),
        check_vma=False,
    )
```

```python
import functools

import jax
import jax.numpy as jnp
from jax import lax
from jax.experimental import pallas as pl
from jax.experimental.pallas import tpu as pltpu
from jax.sharding import PartitionSpec as P

TILE = 128
CAP = 16
HALF = 128
MESH = pl.DeviceIdType.MESH
BF16 = jnp.bfloat16
F32 = jnp.float32
SUB_WIRE = jnp.float32
G_WIRE = jnp.bfloat16
KEEP_BYTES = 16 << 20
PIECES = 2


def kernel(n, n_rep, n_sub, halves, keep,
           og_any, pa_any, tr_any, tc_any, cnt_any, feat_any, w_any, tiles_any,
           fg, gw,
           og, pa, tr, tc, cnt,
           gath, dense, tiles, inv_v, inv_s, part, sub_out, sub_in, rep_out, rep_in, acc, prop,
           feat, feat_t, w, part_b, g1_out, g1_in, zbuf, gfin,
           loc_sem, ssem, rsem, sub_ss, sub_rs, rep_ss, rep_rs, ft_ss, ft_rs, g1_ss, g1_rs, z_ss, z_rs, f_ss, f_rs):
    rows = og_any.shape[0]
    slots = tiles_any.shape[0]
    shard = rows // TILE
    members = n_rep * n_sub
    strip = members * rows
    strip_tiles = strip // TILE
    b = lax.axis_index("blk")
    r = lax.axis_index("rep")
    s = lax.axis_index("sub")
    m = r * n_sub + s
    piece = feat_any.shape[1] // members
    span = rows // PIECES

    def member(t):
        return {"rep": t // n_sub, "sub": lax.rem(t, n_sub)}

    og_copy = pltpu.make_async_copy(og_any, og, loc_sem.at[4])
    pa_copy = pltpu.make_async_copy(pa_any, pa, loc_sem.at[5])
    list_copies = [
        pltpu.make_async_copy(source, kept, loc_sem.at[6 + i])
        for i, (source, kept) in enumerate(((tr_any, tr), (tc_any, tc), (cnt_any, cnt)))
    ]
    og_copy.start()
    pa_copy.start()
    for copy in list_copies:
        copy.start()

    barrier = pltpu.get_barrier_semaphore()
    for o in range(1, n):
        pl.semaphore_signal(barrier, inc=1, device_id={"blk": lax.rem(b + o, n)}, device_id_type=MESH)
    for o in range(1, members):
        pl.semaphore_signal(barrier, inc=1, device_id=member(lax.rem(m + o, members)), device_id_type=MESH)

    tiles_copy = pltpu.make_async_copy(tiles_any, tiles.at[pl.ds(0, slots)], loc_sem.at[0])
    feat_copy = pltpu.make_async_copy(feat_any, feat, loc_sem.at[1])
    w_copy = pltpu.make_async_copy(w_any, w, loc_sem.at[2])
    tiles_copy.start()
    feat_copy.start()
    w_copy.start()

    og_copy.wait()
    pa_copy.wait()
    for c in range(halves):
        cols = pl.ds(c * HALF, HALF)
        x = og[:, cols]
        gath[b, c] = jnp.where(pa[:, cols] > 0, x, jnp.zeros_like(x))

    def block_copy(c, p, origin, way):
        at = pl.ds(p * span, span)
        return pltpu.make_async_remote_copy(
            src_ref=gath.at[origin, c, at], dst_ref=gath.at[origin, c, at],
            send_sem=ssem.at[way, origin, c, p], recv_sem=rsem.at[origin, c, p],
            device_id={"blk": jnp.clip(b + (1 if way else -1), 0, n - 1)}, device_id_type=MESH)

    def send(c, p, origin, way):
        @pl.when((b + 1 < n) if way else (b > 0))
        def _():
            block_copy(c, p, origin, way).start()

    def send_own(c):
        for p in range(PIECES):
            send(c, p, b, 0)
            send(c, p, b, 1)

    def feat_send(o):
        return pltpu.make_async_remote_copy(
            src_ref=feat_t.at[m], dst_ref=feat_t.at[m],
            send_sem=ft_ss.at[o - 1], recv_sem=ft_rs.at[m],
            device_id=member(lax.rem(m + o, members)), device_id_type=MESH)

    def feat_recv(o):
        origin = lax.rem(m + o, members)
        return pltpu.make_async_remote_copy(
            src_ref=feat_t.at[origin], dst_ref=feat_t.at[origin],
            send_sem=ft_ss.at[o - 1], recv_sem=ft_rs.at[origin],
            device_id=member(origin), device_id_type=MESH)

    pl.semaphore_wait(barrier, n - 1 + members - 1)
    send_own(0)
    feat_copy.wait()
    feat_t[m] = feat[...].T
    for o in range(1, members):
        feat_send(o).start()

    for copy in list_copies:
        copy.wait()

    lane = lax.broadcasted_iota(jnp.int32, (1, inv_v.shape[1]), 1)

    def invert(g, carry):
        v = jnp.full((1, inv_v.shape[1]), slots, jnp.int32)
        for k in range(CAP):
            slot = g * CAP + k
            key = jnp.where(k < cnt[g], tr[slot] * shard + tc[slot], -1)
            v = jnp.where(lane == key, slot, v)
        inv_v[pl.ds(g, 1), :] = v
        return carry

    lax.fori_loop(0, n, invert, 0)
    inv_copy = pltpu.make_async_copy(inv_v, inv_s, loc_sem.at[3])
    inv_copy.start()
    tiles[slots] = jnp.zeros((TILE, TILE), BF16)
    inv_copy.wait()
    tiles_copy.wait()

    def build(g):
        where = g if keep else 0

        def one(t, carry):
            for c in range(shard):
                index = inv_s[g, t * shard + c]
                dense[where, pl.ds(pl.multiple_of(t * TILE, TILE), TILE), pl.ds(c * TILE, TILE)] = tiles[index]
            return carry

        lax.fori_loop(0, strip_tiles, one, 0)

    def accumulate(g, c, first):
        where = g if keep else 0
        if c == 0 or not keep:
            build(g)
        step = 512

        def one(t, carry):
            at = pl.ds(pl.multiple_of(t * step, step), step)
            product = jnp.dot(dense[where, at, :], gath[g, c], preferred_element_type=F32)
            if first:
                part[c, at, :] = product
            else:
                part[c, at, :] += product
            return carry

        lax.fori_loop(0, strip // step, one, 0)

    def gather(c, low, high):
        def one(d, carry):
            for p in range(PIECES):
                @pl.when(b - d >= 0)
                def _():
                    block_copy(c, p, b - d, 1).wait_recv()
                    send(c, p, b - d, 1)

                @pl.when(b + d < n)
                def _():
                    block_copy(c, p, b + d, 0).wait_recv()
                    send(c, p, b + d, 0)

            if c + 1 < halves:
                @pl.when(d == 1)
                def _():
                    send_own(c + 1)

            @pl.when(b - d >= 0)
            def _():
                accumulate(b - d, c, False)

            @pl.when(b + d < n)
            def _():
                accumulate(b + d, c, False)
            return carry

        if low < high:
            lax.fori_loop(low, high, one, 0)

    def sub_copy(c, o, q):
        at = pl.ds(pl.multiple_of(q * rows, rows), rows)
        return pltpu.make_async_remote_copy(
            src_ref=sub_out.at[c, o - 1, at], dst_ref=sub_in.at[c, o - 1, at],
            send_sem=sub_ss.at[c, o - 1, q], recv_sem=sub_rs.at[c, o - 1, q],
            device_id={"sub": lax.rem(s + o, n_sub)}, device_id_type=MESH)

    def rep_copy(c, o):
        return pltpu.make_async_remote_copy(
            src_ref=rep_out.at[c, o - 1], dst_ref=rep_in.at[c, o - 1],
            send_sem=rep_ss.at[c, o - 1], recv_sem=rep_rs.at[c, o - 1],
            device_id={"rep": lax.rem(r + o, n_rep)}, device_id_type=MESH)

    def block_rows(t):
        return pl.ds(pl.multiple_of(t * rows, rows), rows)

    def sub_stage(c):
        for p in range(1, n_rep + 1):
            q = lax.rem(r + p, n_rep)
            for o in range(1, n_sub):
                t = lax.rem(s + o, n_sub)
                sub_out[c, o - 1, block_rows(q), :] = part[c, block_rows(q * n_sub + t), :].astype(SUB_WIRE)
                sub_copy(c, o, q).start()

    def rep_stage(c):
        def summed(t):
            total = part[c, block_rows(t * n_sub + s), :]
            for o in range(1, n_sub):
                sub_copy(c, o, t).wait_recv()
                total = total + sub_in[c, o - 1, block_rows(t), :].astype(F32)
            return total

        for o in range(1, n_rep):
            rep_out[c, o - 1] = summed(lax.rem(r + o, n_rep)).astype(BF16)
            rep_copy(c, o).start()
        acc[c] = summed(r)

    def prop_stage(c):
        total = acc[c]
        for o in range(1, n_rep):
            rep_copy(c, o).wait_recv()
            total = total + rep_in[c, o - 1].astype(F32)
        prop[c] = total.astype(BF16)

    def g1_copy(c, o):
        return pltpu.make_async_remote_copy(
            src_ref=g1_out.at[c, lax.rem(m + o, members)], dst_ref=g1_in.at[c, o - 1],
            send_sem=g1_ss.at[c, o - 1], recv_sem=g1_rs.at[c, o - 1],
            device_id=member(lax.rem(m + o, members)), device_id_type=MESH)

    def z_copy(c, o, origin):
        return pltpu.make_async_remote_copy(
            src_ref=zbuf.at[c, origin], dst_ref=zbuf.at[c, origin],
            send_sem=z_ss.at[c, o - 1], recv_sem=z_rs.at[c, origin],
            device_id={"blk": lax.rem(b + o, n)}, device_id_type=MESH)

    def f_copy(c, o, origin):
        return pltpu.make_async_remote_copy(
            src_ref=gfin.at[c, origin], dst_ref=gfin.at[c, origin],
            send_sem=f_ss.at[c, o - 1], recv_sem=f_rs.at[c, origin],
            device_id=member(lax.rem(m + o, members)), device_id_type=MESH)

    def weight_term(c):
        if c == 0:
            for o in range(1, members):
                feat_recv(o).wait_recv()
        total = None
        for q in range(members):
            part_b[...] = part[c, pl.ds(q * rows, rows), :].astype(BF16)
            term = jnp.dot(feat_t[q], part_b[...], preferred_element_type=F32)
            total = term if total is None else total + term
        for q in range(members):
            g1_out[c, q] = total[q * piece:(q + 1) * piece].astype(G_WIRE)
        for o in range(1, members):
            g1_copy(c, o).start()

    def strips_stage(c):
        total = g1_out[c, m].astype(F32)
        for o in range(1, members):
            g1_copy(c, o).wait_recv()
            total = total + g1_in[c, o - 1].astype(F32)
        zbuf[c, b] = total.astype(G_WIRE)
        for o in range(1, n):
            z_copy(c, o, b).start()

    def back_stage(c):
        for o in range(1, n):
            z_copy(c, o, lax.rem(b + o, n)).wait_recv()
        total = zbuf[c, 0].astype(F32)
        for q in range(1, n):
            total = total + zbuf[c, q].astype(F32)
        gfin[c, m] = total.astype(G_WIRE)
        for o in range(1, members):
            f_copy(c, o, m).start()

    def weight_out(c):
        for o in range(1, members):
            f_copy(c, o, lax.rem(m + o, members)).wait_recv()
        for q in range(members):
            gw[pl.ds(q * piece, piece), pl.ds(c * HALF, HALF)] = gfin[c, q].astype(F32)

    def feature_out():
        total = None
        for c in range(halves):
            term = lax.dot_general(prop[c], w[:, pl.ds(c * HALF, HALF)], (((1,), (1,)), ((), ())),
                                   preferred_element_type=F32)
            total = term if total is None else total + term
        fg[...] = total.astype(BF16)

    accumulate(b, 0, True)
    gather(0, 1, n)
    for c in range(halves):
        sub_stage(c)
        weight_term(c)
        if c + 1 < halves:
            accumulate(b, c + 1, True)
            gather(c + 1, 1, 2)
            rep_stage(c)
            strips_stage(c)
            gather(c + 1, 2, 3)
            prop_stage(c)
            back_stage(c)
            gather(c + 1, 3, n)
        else:
            rep_stage(c)
            strips_stage(c)
            prop_stage(c)
            w_copy.wait()
            feature_out()
            back_stage(c)
        if c > 0:
            weight_out(c - 1)
    weight_out(halves - 1)

    def drain(origin, carry):
        for c in range(halves):
            for p in range(PIECES):
                @pl.when((origin <= b) & (b + 1 < n))
                def _():
                    block_copy(c, p, origin, 1).wait_send()

                @pl.when((origin >= b) & (b > 0))
                def _():
                    block_copy(c, p, origin, 0).wait_send()
        return carry

    lax.fori_loop(0, n, drain, 0)
    for o in range(1, members):
        feat_send(o).wait_send()
    for c in range(halves):
        for o in range(1, n_sub):
            for q in range(n_rep):
                sub_copy(c, o, q).wait_send()
        for o in range(1, n_rep):
            rep_copy(c, o).wait_send()
        for o in range(1, members):
            g1_copy(c, o).wait_send()
            f_copy(c, o, m).wait_send()
        for o in range(1, n):
            z_copy(c, o, b).wait_send()


def local(n, n_rep, n_sub, out_grad, pre_act, features, weight, prop_tiles, tile_rows, tile_cols, tile_counts):
    rows, width = out_grad.shape
    f_in = features.shape[1]
    slots = prop_tiles.shape[0]
    halves = width // HALF
    members = n_rep * n_sub
    strip = members * rows
    keep = n * strip * rows * 2 <= KEEP_BYTES
    lanes = -(-(strip // TILE) * (rows // TILE) // 128) * 128
    inv_shape = (-(-n // 8) * 8, lanes)
    piece = f_in // members
    dma = pltpu.SemaphoreType.DMA
    vmem = pl.BlockSpec(memory_space=pltpu.VMEM)
    hbm = pl.BlockSpec(memory_space=pltpu.HBM)
    subs, reps = max(n_sub - 1, 1), max(n_rep - 1, 1)
    return pl.pallas_call(
        functools.partial(kernel, n, n_rep, n_sub, halves, keep),
        out_shape=(
            jax.ShapeDtypeStruct((rows, weight.shape[0]), BF16),
            jax.ShapeDtypeStruct((f_in, width), F32),
        ),
        in_specs=[hbm] * 8,
        out_specs=(vmem, vmem),
        scratch_shapes=[
            pltpu.VMEM(out_grad.shape, BF16),
            pltpu.VMEM(pre_act.shape, BF16),
            pltpu.SMEM(tile_rows.shape, jnp.int32),
            pltpu.SMEM(tile_cols.shape, jnp.int32),
            pltpu.SMEM(tile_counts.shape, jnp.int32),
            pltpu.VMEM((n, halves, rows, HALF), BF16),
            pltpu.VMEM((n if keep else 1, strip, rows), BF16),
            pltpu.VMEM((slots + 1, TILE, TILE), BF16),
            pltpu.VMEM(inv_shape, jnp.int32),
            pltpu.SMEM(inv_shape, jnp.int32),
            pltpu.VMEM((halves, strip, HALF), F32),
            pltpu.VMEM((halves, subs, n_rep * rows, HALF), SUB_WIRE),
            pltpu.VMEM((halves, subs, n_rep * rows, HALF), SUB_WIRE),
            pltpu.VMEM((halves, reps, rows, HALF), BF16),
            pltpu.VMEM((halves, reps, rows, HALF), BF16),
            pltpu.VMEM((halves, rows, HALF), F32),
            pltpu.VMEM((halves, rows, HALF), BF16),
            pltpu.VMEM(features.shape, BF16),
            pltpu.VMEM((members, f_in, rows), BF16),
            pltpu.VMEM(weight.shape, BF16),
            pltpu.VMEM((rows, HALF), BF16),
            pltpu.VMEM((halves, members, piece, HALF), G_WIRE),
            pltpu.VMEM((halves, members - 1, piece, HALF), G_WIRE),
            pltpu.VMEM((halves, n, piece, HALF), G_WIRE),
            pltpu.VMEM((halves, members, piece, HALF), G_WIRE),
            dma((9,)),
            dma((2, n, halves, PIECES)),
            dma((n, halves, PIECES)),
            dma((halves, subs, n_rep)),
            dma((halves, subs, n_rep)),
            dma((halves, reps)),
            dma((halves, reps)),
            dma((members - 1,)),
            dma((members,)),
            dma((halves, members - 1)),
            dma((halves, members - 1)),
            dma((halves, n - 1)),
            dma((halves, n)),
            dma((halves, members - 1)),
            dma((halves, members)),
        ],
        compiler_params=pltpu.CompilerParams(
            collective_id=0, has_side_effects=True, vmem_limit_bytes=64 << 20),
    )(out_grad, pre_act, tile_rows, tile_cols, tile_counts, features, weight, prop_tiles)


def solution(mesh):
    placed = P(("groups", "blk", "rep", "sub"))
    return jax.shard_map(
        functools.partial(local, mesh.shape["blk"], mesh.shape["rep"], mesh.shape["sub"]),
        mesh=mesh,
        in_specs=(placed, placed, placed, P(), placed, placed, placed, placed),
        out_specs=(placed, P("groups", None)),
        check_vma=False,
    )
```

```python
import functools

import jax
import jax.numpy as jnp
from jax import lax
from jax.experimental import pallas as pl
from jax.experimental.pallas import tpu as pltpu
from jax.sharding import PartitionSpec as P

TILE = 128
CAP = 16
HALF = 128
MESH = pl.DeviceIdType.MESH
BF16 = jnp.bfloat16
F32 = jnp.float32
SUB_WIRE = jnp.float32
G_WIRE = jnp.bfloat16
KEEP_BYTES = 16 << 20
PIECES = 2
STEP = 2048


def kernel(n, n_rep, n_sub, halves, keep,
           og_any, pa_any, tr_any, tc_any, cnt_any, feat_any, tiles_any,
           prop, weight_sums,
           og, pa, tr, tc, cnt,
           gath, dense, tiles, inv_v, inv_s, part, sub_out, sub_in, rep_out, rep_in, acc,
           feat, feat_t, part_b, g1_out, g1_in, zbuf, gfin,
           loc_sem, ssem, rsem, sub_ss, sub_rs, rep_ss, rep_rs, ft_ss, ft_rs, g1_ss, g1_rs, z_ss, z_rs, f_ss, f_rs):
    rows = og_any.shape[0]
    slots = tiles_any.shape[0]
    shard = rows // TILE
    members = n_rep * n_sub
    strip = members * rows
    strip_tiles = strip // TILE
    b = lax.axis_index("blk")
    r = lax.axis_index("rep")
    s = lax.axis_index("sub")
    m = r * n_sub + s
    piece = feat_any.shape[1] // members
    span = rows // PIECES

    def member(t):
        return {"rep": t // n_sub, "sub": lax.rem(t, n_sub)}

    og_copy = pltpu.make_async_copy(og_any, og, loc_sem.at[4])
    pa_copy = pltpu.make_async_copy(pa_any, pa, loc_sem.at[5])
    list_copies = [
        pltpu.make_async_copy(source, kept, loc_sem.at[6 + i])
        for i, (source, kept) in enumerate(((tr_any, tr), (tc_any, tc), (cnt_any, cnt)))
    ]
    og_copy.start()
    pa_copy.start()
    for copy in list_copies:
        copy.start()

    barrier = pltpu.get_barrier_semaphore()
    for o in range(1, n):
        pl.semaphore_signal(barrier, inc=1, device_id={"blk": lax.rem(b + o, n)}, device_id_type=MESH)
    for o in range(1, members):
        pl.semaphore_signal(barrier, inc=1, device_id=member(lax.rem(m + o, members)), device_id_type=MESH)

    tiles_copy = pltpu.make_async_copy(tiles_any, tiles.at[pl.ds(0, slots)], loc_sem.at[0])
    feat_copy = pltpu.make_async_copy(feat_any, feat, loc_sem.at[1])
    tiles_copy.start()
    feat_copy.start()

    og_copy.wait()
    pa_copy.wait()
    for c in range(halves):
        cols = pl.ds(c * HALF, HALF)
        x = og[:, cols]
        gath[b, c] = jnp.where(pa[:, cols] > 0, x, jnp.zeros_like(x))

    def block_copy(c, p, origin, way):
        at = pl.ds(p * span, span)
        return pltpu.make_async_remote_copy(
            src_ref=gath.at[origin, c, at], dst_ref=gath.at[origin, c, at],
            send_sem=ssem.at[way, origin, c, p], recv_sem=rsem.at[origin, c, p],
            device_id={"blk": jnp.clip(b + (1 if way else -1), 0, n - 1)}, device_id_type=MESH)

    def send(c, p, origin, way):
        @pl.when((b + 1 < n) if way else (b > 0))
        def _():
            block_copy(c, p, origin, way).start()

    def send_own(c):
        for p in range(PIECES):
            send(c, p, b, 0)
            send(c, p, b, 1)

    def feat_send(o):
        return pltpu.make_async_remote_copy(
            src_ref=feat_t.at[m], dst_ref=feat_t.at[m],
            send_sem=ft_ss.at[o - 1], recv_sem=ft_rs.at[m],
            device_id=member(lax.rem(m + o, members)), device_id_type=MESH)

    def feat_recv(o):
        origin = lax.rem(m + o, members)
        return pltpu.make_async_remote_copy(
            src_ref=feat_t.at[origin], dst_ref=feat_t.at[origin],
            send_sem=ft_ss.at[o - 1], recv_sem=ft_rs.at[origin],
            device_id=member(origin), device_id_type=MESH)

    pl.semaphore_wait(barrier, n - 1 + members - 1)
    send_own(0)
    feat_copy.wait()
    feat_t[m] = feat[...].T
    for o in range(1, members):
        feat_send(o).start()

    for copy in list_copies:
        copy.wait()

    lane = lax.broadcasted_iota(jnp.int32, (1, inv_v.shape[1]), 1)

    def invert(g, carry):
        v = jnp.full((1, inv_v.shape[1]), slots, jnp.int32)
        for k in range(CAP):
            slot = g * CAP + k
            key = jnp.where(k < cnt[g], tr[slot] * shard + tc[slot], -1)
            v = jnp.where(lane == key, slot, v)
        inv_v[pl.ds(g, 1), :] = v
        return carry

    lax.fori_loop(0, n, invert, 0)
    inv_copy = pltpu.make_async_copy(inv_v, inv_s, loc_sem.at[3])
    inv_copy.start()
    tiles[slots] = jnp.zeros((TILE, TILE), BF16)
    inv_copy.wait()
    tiles_copy.wait()

    def build(g):
        where = g if keep else 0

        def one(t, carry):
            for c in range(shard):
                index = inv_s[g, t * shard + c]
                dense[where, pl.ds(pl.multiple_of(t * TILE, TILE), TILE), pl.ds(c * TILE, TILE)] = tiles[index]
            return carry

        lax.fori_loop(0, strip_tiles, one, 0)

    def accumulate(g, c, first):
        where = g if keep else 0
        if c == 0 or not keep:
            build(g)

        def one(t, carry):
            at = pl.ds(pl.multiple_of(t * STEP, STEP), STEP)
            product = jnp.dot(dense[where, at, :], gath[g, c], preferred_element_type=F32)
            if first:
                part[c, at, :] = product
            else:
                part[c, at, :] += product
            return carry

        lax.fori_loop(0, strip // STEP, one, 0)

    def gather(c, low, high):
        def one(d, carry):
            for p in range(PIECES):
                @pl.when(b - d >= 0)
                def _():
                    block_copy(c, p, b - d, 1).wait_recv()
                    send(c, p, b - d, 1)

                @pl.when(b + d < n)
                def _():
                    block_copy(c, p, b + d, 0).wait_recv()
                    send(c, p, b + d, 0)

            if c + 1 < halves:
                @pl.when(d == 1)
                def _():
                    send_own(c + 1)

            @pl.when(b - d >= 0)
            def _():
                accumulate(b - d, c, False)

            @pl.when(b + d < n)
            def _():
                accumulate(b + d, c, False)
            return carry

        if low < high:
            lax.fori_loop(low, high, one, 0)

    def sub_copy(c, o, q):
        at = pl.ds(pl.multiple_of(q * rows, rows), rows)
        return pltpu.make_async_remote_copy(
            src_ref=sub_out.at[c, o - 1, at], dst_ref=sub_in.at[c, o - 1, at],
            send_sem=sub_ss.at[c, o - 1, q], recv_sem=sub_rs.at[c, o - 1, q],
            device_id={"sub": lax.rem(s + o, n_sub)}, device_id_type=MESH)

    def rep_copy(c, o):
        return pltpu.make_async_remote_copy(
            src_ref=rep_out.at[c, o - 1], dst_ref=rep_in.at[c, o - 1],
            send_sem=rep_ss.at[c, o - 1], recv_sem=rep_rs.at[c, o - 1],
            device_id={"rep": lax.rem(r + o, n_rep)}, device_id_type=MESH)

    def block_rows(t):
        return pl.ds(pl.multiple_of(t * rows, rows), rows)

    def sub_stage(c):
        for p in range(1, n_rep + 1):
            q = lax.rem(r + p, n_rep)
            for o in range(1, n_sub):
                t = lax.rem(s + o, n_sub)
                sub_out[c, o - 1, block_rows(q), :] = part[c, block_rows(q * n_sub + t), :].astype(SUB_WIRE)
                sub_copy(c, o, q).start()

    def rep_stage(c):
        def summed(t):
            total = part[c, block_rows(t * n_sub + s), :]
            for o in range(1, n_sub):
                sub_copy(c, o, t).wait_recv()
                total = total + sub_in[c, o - 1, block_rows(t), :].astype(F32)
            return total

        for o in range(1, n_rep):
            rep_out[c, o - 1] = summed(lax.rem(r + o, n_rep)).astype(BF16)
            rep_copy(c, o).start()
        acc[c] = summed(r)

    def prop_stage(c):
        total = acc[c]
        for o in range(1, n_rep):
            rep_copy(c, o).wait_recv()
            total = total + rep_in[c, o - 1].astype(F32)
        prop[:, pl.ds(c * HALF, HALF)] = total.astype(BF16)

    def g1_copy(c, o):
        return pltpu.make_async_remote_copy(
            src_ref=g1_out.at[c, lax.rem(m + o, members)], dst_ref=g1_in.at[c, o - 1],
            send_sem=g1_ss.at[c, o - 1], recv_sem=g1_rs.at[c, o - 1],
            device_id=member(lax.rem(m + o, members)), device_id_type=MESH)

    def z_copy(c, o, origin):
        return pltpu.make_async_remote_copy(
            src_ref=zbuf.at[c, origin], dst_ref=zbuf.at[c, origin],
            send_sem=z_ss.at[c, o - 1], recv_sem=z_rs.at[c, origin],
            device_id={"blk": lax.rem(b + o, n)}, device_id_type=MESH)

    def f_copy(c, o, origin):
        return pltpu.make_async_remote_copy(
            src_ref=gfin.at[c, origin], dst_ref=gfin.at[c, origin],
            send_sem=f_ss.at[c, o - 1], recv_sem=f_rs.at[c, origin],
            device_id=member(lax.rem(m + o, members)), device_id_type=MESH)

    def weight_term(c):
        if c == 0:
            for o in range(1, members):
                feat_recv(o).wait_recv()
        total = None
        for q in range(members):
            part_b[...] = part[c, pl.ds(q * rows, rows), :].astype(BF16)
            term = jnp.dot(feat_t[q], part_b[...], preferred_element_type=F32)
            total = term if total is None else total + term
        for q in range(members):
            g1_out[c, q] = total[q * piece:(q + 1) * piece].astype(G_WIRE)
        for o in range(1, members):
            g1_copy(c, o).start()

    def strips_stage(c):
        total = g1_out[c, m].astype(F32)
        for o in range(1, members):
            g1_copy(c, o).wait_recv()
            total = total + g1_in[c, o - 1].astype(F32)
        zbuf[c, b] = total.astype(G_WIRE)
        for o in range(1, n):
            z_copy(c, o, b).start()

    def back_stage(c):
        for o in range(1, n):
            z_copy(c, o, lax.rem(b + o, n)).wait_recv()
        total = zbuf[c, 0].astype(F32)
        for q in range(1, n):
            total = total + zbuf[c, q].astype(F32)
        gfin[c, m] = total.astype(G_WIRE)
        for o in range(1, members):
            f_copy(c, o, m).start()

    def weight_out(c):
        for o in range(1, members):
            f_copy(c, o, lax.rem(m + o, members)).wait_recv()
        for q in range(members):
            weight_sums[pl.ds(q * piece, piece), pl.ds(c * HALF, HALF)] = gfin[c, q]

    accumulate(b, 0, True)
    gather(0, 1, n)
    for c in range(halves):
        sub_stage(c)
        weight_term(c)
        if c > 0:
            back_stage(c - 1)
        if c + 1 < halves:
            accumulate(b, c + 1, True)
            gather(c + 1, 1, 3)
            rep_stage(c)
            strips_stage(c)
            gather(c + 1, 3, n)
        else:
            rep_stage(c)
            strips_stage(c)
            back_stage(c)
            for q in range(halves):
                prop_stage(q)
    for c in range(halves):
        weight_out(c)

    def drain(origin, carry):
        for c in range(halves):
            for p in range(PIECES):
                @pl.when((origin <= b) & (b + 1 < n))
                def _():
                    block_copy(c, p, origin, 1).wait_send()

                @pl.when((origin >= b) & (b > 0))
                def _():
                    block_copy(c, p, origin, 0).wait_send()
        return carry

    lax.fori_loop(0, n, drain, 0)
    for o in range(1, members):
        feat_send(o).wait_send()
    for c in range(halves):
        for o in range(1, n_sub):
            for q in range(n_rep):
                sub_copy(c, o, q).wait_send()
        for o in range(1, n_rep):
            rep_copy(c, o).wait_send()
        for o in range(1, members):
            g1_copy(c, o).wait_send()
            f_copy(c, o, m).wait_send()
        for o in range(1, n):
            z_copy(c, o, b).wait_send()


def finish(prop, w, weight_sums, fg, gw):
    fg[...] = lax.dot_general(prop[...], w[...], (((1,), (1,)), ((), ())),
                              preferred_element_type=F32).astype(BF16)
    gw[...] = weight_sums[...].astype(F32)


def local(n, n_rep, n_sub, out_grad, pre_act, features, weight, prop_tiles, tile_rows, tile_cols, tile_counts):
    rows, width = out_grad.shape
    f_in = features.shape[1]
    slots = prop_tiles.shape[0]
    halves = width // HALF
    members = n_rep * n_sub
    strip = members * rows
    keep = n * strip * rows * 2 <= KEEP_BYTES
    lanes = -(-(strip // TILE) * (rows // TILE) // 128) * 128
    inv_shape = (-(-n // 8) * 8, lanes)
    piece = f_in // members
    dma = pltpu.SemaphoreType.DMA
    vmem = pl.BlockSpec(memory_space=pltpu.VMEM)
    hbm = pl.BlockSpec(memory_space=pltpu.HBM)
    subs, reps = max(n_sub - 1, 1), max(n_rep - 1, 1)
    prop, weight_sums = pl.pallas_call(
        functools.partial(kernel, n, n_rep, n_sub, halves, keep),
        out_shape=(
            jax.ShapeDtypeStruct((rows, width), BF16),
            jax.ShapeDtypeStruct((f_in, width), G_WIRE),
        ),
        in_specs=[hbm] * 7,
        out_specs=(vmem, vmem),
        scratch_shapes=[
            pltpu.VMEM(out_grad.shape, BF16),
            pltpu.VMEM(pre_act.shape, BF16),
            pltpu.SMEM(tile_rows.shape, jnp.int32),
            pltpu.SMEM(tile_cols.shape, jnp.int32),
            pltpu.SMEM(tile_counts.shape, jnp.int32),
            pltpu.VMEM((n, halves, rows, HALF), BF16),
            pltpu.VMEM((n if keep else 1, strip, rows), BF16),
            pltpu.VMEM((slots + 1, TILE, TILE), BF16),
            pltpu.VMEM(inv_shape, jnp.int32),
            pltpu.SMEM(inv_shape, jnp.int32),
            pltpu.VMEM((halves, strip, HALF), F32),
            pltpu.VMEM((halves, subs, n_rep * rows, HALF), SUB_WIRE),
            pltpu.VMEM((halves, subs, n_rep * rows, HALF), SUB_WIRE),
            pltpu.VMEM((halves, reps, rows, HALF), BF16),
            pltpu.VMEM((halves, reps, rows, HALF), BF16),
            pltpu.VMEM((halves, rows, HALF), F32),
            pltpu.VMEM(features.shape, BF16),
            pltpu.VMEM((members, f_in, rows), BF16),
            pltpu.VMEM((rows, HALF), BF16),
            pltpu.VMEM((halves, members, piece, HALF), G_WIRE),
            pltpu.VMEM((halves, members - 1, piece, HALF), G_WIRE),
            pltpu.VMEM((halves, n, piece, HALF), G_WIRE),
            pltpu.VMEM((halves, members, piece, HALF), G_WIRE),
            dma((9,)),
            dma((2, n, halves, PIECES)),
            dma((n, halves, PIECES)),
            dma((halves, subs, n_rep)),
            dma((halves, subs, n_rep)),
            dma((halves, reps)),
            dma((halves, reps)),
            dma((members - 1,)),
            dma((members,)),
            dma((halves, members - 1)),
            dma((halves, members - 1)),
            dma((halves, n - 1)),
            dma((halves, n)),
            dma((halves, members - 1)),
            dma((halves, members)),
        ],
        compiler_params=pltpu.CompilerParams(
            collective_id=0, has_side_effects=True, vmem_limit_bytes=64 << 20),
    )(out_grad, pre_act, tile_rows, tile_cols, tile_counts, features, prop_tiles)
    return pl.pallas_call(
        finish,
        out_shape=(
            jax.ShapeDtypeStruct((rows, weight.shape[0]), BF16),
            jax.ShapeDtypeStruct((f_in, width), F32),
        ),
        in_specs=[vmem] * 3,
        out_specs=(vmem, vmem),
    )(prop, weight, weight_sums)


def solution(mesh):
    placed = P(("groups", "blk", "rep", "sub"))
    return jax.shard_map(
        functools.partial(local, mesh.shape["blk"], mesh.shape["rep"], mesh.shape["sub"]),
        mesh=mesh,
        in_specs=(placed, placed, placed, P(), placed, placed, placed, placed),
        out_specs=(placed, P("groups", None)),
        check_vma=False,
    )
```
